32 devices in a mesh: space: 8 (over z, y), scene: 4 (over x, core).
Axes of the slice: x: 2, y: 2, z: 4, core: 2. Of those that a mesh axis runs over, the one named last changes fastest.
Arguments:
- features: bfloat16 [4, 16, 8, 8, 8, 256], P('scene', 'space'), may hold values from -6 to 6
- cotangent: bfloat16 [4, 16, 8, 8, 8, 256], P('scene', 'space'), may hold values from -6 to 6
- weight: bfloat16 [27, 256, 256], replicated, may hold values from -0.078125 to 0.078125
- counts: int32 [4, 8], P('scene', 'space'), may hold values from 1 to 2, as said below
- neighbours: int32 [4, 16, 26], P('scene', 'space'), may hold values from -1 to 15, as said below
- occupancy: int32 [4, 16, 512], P('scene', 'space'), may hold values 0 or 1
Outputs:
- outputs: bfloat16 [4, 16, 8, 8, 8, 256], P('scene', 'space')
- input_grad: bfloat16 [4, 16, 8, 8, 8, 256], P('scene', 'space')
- weight_grad: float32 [27, 256, 256], P(None, 'space', 'scene')
The draws below stay inside these ranges and needn't reach their ends.
Inputs may be any that keep to these rules, and one draw needn't show every extreme that they name: Slots p * 2 to p * 2 + 1 of a scene form partition p; its first counts[s, p] slots are live. In every scene some partition has exactly 2 live slots. `neighbours`: an entry is -1 or the slot number of a live brick of the same scene in the same partition or the partition next to it; only live bricks have entries other than -1. The lists are symmetric: if brick a names brick c in direction d, brick c names brick a in the opposite direction.
All inputs are finite; a program needn't handle non-finite values. No bound on the sum of `occupancy` on one device may be relied on, other than what follows from the above.
Results may differ from the reference program's by a relative error of at most 0.001.
Values may be sent and summed in bfloat16 or wider, within the bound.
A program may use at most 128 MiB of HBM per device.

```python
import jax
import jax.numpy as jnp
from jax import lax

CHANNELS = 256
EDGE = 8
VOXELS = 512
TAPS = 27
B_DEV = 2
PARTITIONS = 8
BRICKS = 16
SCENES = 4


def brick_counts(key):
    drawn_counts = jax.random.randint(jax.random.fold_in(key, 101), (SCENES, PARTITIONS), 1, B_DEV + 1)
    chosen = jax.random.randint(jax.random.fold_in(key, 102), (SCENES, 1), 0, PARTITIONS)
    forced = jnp.arange(PARTITIONS)[None, :] == chosen
    return jnp.where(forced, B_DEV, drawn_counts).astype(jnp.int32)


def draw_counts(key, part):
    return brick_counts(key)


def draw_neighbours(key, part):
    counts_table = brick_counts(key)
    key = jax.random.fold_in(key, 3)
    shift_key, link_key = jax.random.split(key)
    shifts = jax.random.randint(shift_key, (SCENES, 1, 13), 1, B_DEV + 1)
    link_bits = jax.random.randint(link_key, (SCENES, BRICKS, 13), 0, 10) < 7
    brick_ids = jnp.arange(BRICKS, dtype=jnp.int32)
    live_slots = brick_ids[None, :] % B_DEV < jnp.repeat(counts_table, B_DEV, axis=1)
    lower_ids = brick_ids[None, :, None] - shifts
    upper_ids = brick_ids[None, :, None] + shifts
    lower_safe = jnp.clip(lower_ids, 0, BRICKS - 1)
    upper_safe = jnp.clip(upper_ids, 0, BRICKS - 1)

    def lookup_live(where_ids):
        return jnp.take_along_axis(live_slots, where_ids.reshape(SCENES, -1), axis=1).reshape(where_ids.shape)
    lower_ok = link_bits & (lower_ids >= 0) & live_slots[:, :, None] & lookup_live(lower_safe)
    upper_links = jnp.take_along_axis(link_bits, upper_safe, axis=1)
    upper_ok = upper_links & (upper_ids < BRICKS) & live_slots[:, :, None] & lookup_live(upper_safe)
    lower_side = jnp.where(lower_ok, lower_ids, -1)
    upper_side = jnp.where(upper_ok, upper_ids, -1)
    return jnp.concatenate([lower_side, upper_side[:, :, ::-1]], axis=2).astype(jnp.int32)


def touch_ends(array, stream_key, least, top_value):
    spot = [jax.random.randint(jax.random.fold_in(stream_key, axis), (), 0, length) for axis, length in enumerate(array.shape)]
    longest = array.shape.index(max(array.shape))
    next_to = spot[:longest] + [(spot[longest] + 1) % array.shape[longest]] + spot[longest + 1:]
    return array.at[tuple(spot)].set(least).at[tuple(next_to)].set(top_value)


def spiked(array, rng, source, target, blocks, factor):
    owner, partner = [(jnp.arange(array.shape[dim]) // (array.shape[dim] // blocks)).reshape([-1 if axis == dim else 1 for axis in range(array.ndim)]) for dim in (source, target)]
    chosen = jax.random.permutation(rng, blocks)[partner]
    strong = (owner == chosen) | (owner == (partner + blocks // 2) % blocks)
    return jnp.where(strong, factor * array, array)


def block_levels(rng, dims, shards, smallest, top_value):
    def one(axis_at, blocks):
        draws = jax.random.uniform(jax.random.fold_in(jax.random.fold_in(rng, 6), axis_at), (blocks,), jnp.float32, smallest / len(shards), top_value / len(shards))
        return jnp.repeat(jnp.exp(draws), dims[axis_at] // blocks).reshape((-1,) + (1,) * (len(dims) - axis_at - 1))

    level = one(*shards[0])
    for cut in shards[1:]:
        level = level * one(*cut)
    return level


def noise(own_key, dims, spread, bound, pieces=(), kind=jnp.bfloat16):
    result = spread * jax.random.normal(own_key, dims, jnp.float32)
    if pieces:
        result = result * block_levels(own_key, dims, pieces, -0.22, 0.18)
    return jnp.clip(result, -bound, bound).astype(kind)


def noise_with(stream_key, shape, deviation, limit, cuts, heavy, kind=jnp.bfloat16):
    array = deviation * jax.random.normal(stream_key, shape, jnp.float32)
    if cuts:
        array = array * block_levels(stream_key, shape, cuts, -0.22, 0.18)
    return jnp.clip(spiked(array, jax.random.fold_in(stream_key, 3), *heavy), -limit, limit).astype(kind)


def setup_inputs(seed: int = 0) -> dict:
    keys = jax.random.split(jax.random.key(seed), 7)
    features = noise(keys[0], (SCENES, BRICKS, EDGE, EDGE, EDGE, CHANNELS), 1.0, 6.0, ((0, 4), (1, 8)))
    cotangent = noise_with(keys[1], (SCENES, BRICKS, EDGE, EDGE, EDGE, CHANNELS), 1.0, 6.0, ((0, 4), (1, 8)), (1, 5, 8, 2.0))
    weight = noise(keys[2], (TAPS, CHANNELS, CHANNELS), (TAPS * CHANNELS) ** -0.5, 0.078125)
    counts = draw_counts(jax.random.fold_in(keys[6], 71), 0)
    neighbours = draw_neighbours(jax.random.fold_in(keys[6], 71), 0)
    occupancy = touch_ends((jax.random.randint(keys[5], (SCENES, BRICKS, VOXELS), 0, 5) < 3).astype(jnp.int32), jax.random.fold_in(keys[5], 1), 0, 1)
    return dict(features=features, cotangent=cotangent, weight=weight, counts=counts, neighbours=neighbours, occupancy=occupancy)


def boundary(offset, extent):
    if offset < 0:
        return slice(extent - 1, extent)
    if offset == 0:
        return slice(0, extent)
    return slice(0, 1)


def assemble(window, lookup):
    extent = window.shape[1]
    layers = []
    for shift_x in (-1, 0, 1):
        strips = []
        for shift_y in (-1, 0, 1):
            blocks = []
            for shift_z in (-1, 0, 1):
                column = (shift_x + 1) * 9 + (shift_y + 1) * 3 + shift_z + 1
                corner = window[:, boundary(shift_x, extent), boundary(shift_y, extent), boundary(shift_z, extent)]
                blocks.append(jnp.take(corner, lookup[:, column], axis=0))
            strips.append(jnp.concatenate(blocks, axis=3))
        layers.append(jnp.concatenate(strips, axis=2))
    return jnp.concatenate(layers, axis=1)


def offsets():
    return [(shift_x, shift_y, shift_z) for shift_x in (-1, 0, 1) for shift_y in (-1, 0, 1) for shift_z in (-1, 0, 1)]


def window_rows(padded, offset_xyz, extent):
    shift_x, shift_y, shift_z = offset_xyz
    region = padded[:, 1 + shift_x:1 + shift_x + extent, 1 + shift_y:1 + shift_y + extent, 1 + shift_z:1 + shift_z + extent]
    return region.reshape(-1, padded.shape[-1])


def forward_conv(padded, weight, extent):
    summed = None
    for column, offset_xyz in enumerate(offsets()):
        product = jnp.dot(window_rows(padded, offset_xyz, extent), weight[column], preferred_element_type=jnp.float32)
        summed = product if summed is None else summed + product
    return summed


def backward_conv(padded, weight, extent):
    summed = None
    for column, offset_xyz in enumerate(offsets()):
        product = lax.dot_general(window_rows(padded, offset_xyz, extent), weight[26 - column], (((1,), (1,)), ((), ())), preferred_element_type=jnp.float32)
        summed = product if summed is None else summed + product
    return summed


def weight_terms(padded, grad_rows, extent):
    return jnp.stack([lax.dot_general(window_rows(padded, offset_xyz, extent), grad_rows, (((0,), (0,)), ((), ())), preferred_element_type=jnp.float32) for offset_xyz in offsets()])


def reference(features, cotangent, weight, counts, neighbours, occupancy):
    norm_scale = float(SCENES * BRICKS * VOXELS) ** -0.5

    def one_scene(summed, inputs):
        scene_feats, scene_grads, count_row, linked, occupied = inputs
        slot_ids = jnp.arange(BRICKS, dtype=jnp.int32)
        live_slots = (slot_ids % B_DEV < jnp.repeat(count_row, B_DEV)).astype(jnp.int32)
        active = (occupied * live_slots[:, None]).reshape(BRICKS, EDGE, EDGE, EDGE, 1).astype(scene_feats.dtype)
        hidden = jnp.maximum(scene_feats, 0) * active
        masked_grad = scene_grads * active
        brick_ids = jnp.where(linked >= 0, linked, BRICKS).astype(jnp.int32)
        centre = jnp.arange(BRICKS, dtype=jnp.int32)[:, None]
        lookup = jnp.concatenate([brick_ids[:, :13], centre, brick_ids[:, 13:]], axis=1)
        blank_brick = jnp.zeros((1, EDGE, EDGE, EDGE, CHANNELS), scene_feats.dtype)
        padded_hidden = assemble(jnp.concatenate([hidden, blank_brick], axis=0), lookup)
        conv_out = forward_conv(padded_hidden, weight, EDGE).reshape(scene_feats.shape)
        scene_out = ((scene_feats.astype(jnp.float32) + conv_out) * active).astype(jnp.bfloat16)
        padded_grad = assemble(jnp.concatenate([masked_grad, blank_brick], axis=0), lookup)
        hidden_grad = backward_conv(padded_grad, weight, EDGE).reshape(scene_feats.shape)
        scene_input_grad = (masked_grad.astype(jnp.float32) + active * (scene_feats > 0) * hidden_grad).astype(jnp.bfloat16)
        terms = weight_terms(padded_hidden, masked_grad.reshape(-1, CHANNELS), EDGE)
        return summed + norm_scale * terms, (scene_out, scene_input_grad)

    start = jnp.zeros((TAPS, CHANNELS, CHANNELS), jnp.float32)
    weight_grad, (outputs, input_grad) = lax.scan(one_scene, start, (features, cotangent, counts, neighbours, occupancy))
    return outputs, input_grad, weight_grad
```

```python
import functools

import jax
import jax.numpy as jnp
from jax import lax
from jax.experimental import pallas as pl
from jax.experimental.pallas import tpu as pltpu
from jax.sharding import PartitionSpec as P

MESH = pl.DeviceIdType.MESH
VMEM_BYTES = 56 * 1024 * 1024
GROUP = 3


def both_sides(cells):
    count = lax.axis_size("space")
    ends = count - 1
    left = lax.ppermute(cells, "space", [(i, i + 1) for i in range(ends)])
    right = lax.ppermute(cells, "space", [(i + 1, i) for i in range(ends)])
    return left, right


def spans(shift):
    if shift < 0:
        return slice(7, 8), slice(0, 1)
    if shift == 0:
        return slice(0, 8), slice(1, 9)
    return slice(0, 1), slice(9, 10)


def spans_z(shift):
    if shift < 0:
        return slice(7, 8), slice(7, 8)
    if shift == 0:
        return slice(0, 8), slice(8, 16)
    return slice(0, 1), slice(16, 17)


def fill_copies(lookup, bricks, sides, window, staged, copies):
    channels = staged.shape[-1]
    for side, ref in enumerate(sides):
        for b in range(bricks):

            def widen(x, carry, ref=ref, b=b, at=side * bricks + b):
                rows = ref[b, pl.ds(pl.multiple_of(x * 64, 64), 64), :]
                window[at, x] = rows.astype(jnp.float32).reshape(8, 8, channels)
                return carry

            lax.fori_loop(0, 8, widen, 0)
    for b in range(bricks):
        for sx in (-1, 0, 1):
            for sy in (-1, 0, 1):
                for sz in (-1, 0, 1):
                    (from_x, to_x), (from_y, to_y), (from_z, to_z) = spans(sx), spans(sy), spans_z(sz)
                    if sx == sy == sz == 0:
                        staged[to_x, to_y, to_z, :] = window[bricks + b, from_x, from_y, from_z, :]
                        continue
                    at = lookup[b, 9 * (sx + 1) + 3 * (sy + 1) + sz + 1]
                    inside = (at >= 0).astype(jnp.float32)
                    taken = window[jnp.maximum(at, 0), from_x, from_y, from_z, :]
                    staged[to_x, to_y, to_z, :] = taken * inside
        for y in range(3):
            for z in range(3):

                def pack(x, carry, b=b, y=y, z=z):
                    rows = staged[x, y : y + 8, 7 + z : 15 + z, :]
                    copies[y, b, pl.ds(pl.multiple_of(x * 64, 64), 64), z * channels : (z + 1) * channels] = (
                        rows.reshape(64, channels).astype(jnp.bfloat16)
                    )
                    return carry

                lax.fori_loop(0, 10, pack, 0)


def conv_kernel(
    lookup, features, active, hidden_t,
    hid_left, hidden, hid_right, grad_left, grad, grad_right, weight, weight_t,
    outputs, input_grad, terms,
    window, staged, hid_copies, grad_copies, total,
):
    bricks = hidden.shape[0]
    channels = hidden.shape[-1]

    def rows_of(copies, i, b):
        start = pl.multiple_of((i // 3) * 64, 64)
        return copies[i % 3, b, pl.ds(start, 512), :]

    fill_copies(lookup, bricks, (grad_left, grad, grad_right), window, staged, grad_copies)

    def gradient(i, carry):
        for z in range(3):
            summed = None
            for b in range(bricks):
                start = pl.multiple_of((i // 3) * 64, 64)
                rows = grad_copies[i % 3, b, pl.ds(start, 512), z * channels : (z + 1) * channels]
                product = jnp.dot(hidden_t[b], rows, preferred_element_type=jnp.float32)
                summed = product if summed is None else summed + product
            tap = 26 - 3 * i - z
            half = channels // 2
            terms[tap, 0] = summed[:, :half]
            terms[tap, 1] = summed[:, half:]
        return carry

    lax.fori_loop(0, 9, gradient, 0)
    fill_copies(lookup, bricks, (hid_left, hidden, hid_right), window, staged, hid_copies)

    for b in range(bricks):
        for copies, matrix in ((hid_copies, weight), (grad_copies, weight_t)):
            total[...] = jnp.zeros_like(total)

            def step(i, carry, b=b, copies=copies, matrix=matrix):
                total[...] += jnp.dot(rows_of(copies, i, b), matrix[i], preferred_element_type=jnp.float32)
                return carry

            lax.fori_loop(0, 9, step, 0)
            if copies is hid_copies:
                summed = (features[b].astype(jnp.float32) + total[...]) * active[b]
                outputs[b] = summed.astype(jnp.bfloat16)
            else:
                kept = jnp.where(hidden[b].astype(jnp.float32) > 0, total[...], 0.0)
                input_grad[b] = (grad[b].astype(jnp.float32) + kept).astype(jnp.bfloat16)


def convolve(lookup, features, active, hidden_t, hiddens, grads, weight, weight_t):
    bricks, voxels, channels = features.shape
    vmem = pl.BlockSpec(memory_space=pltpu.VMEM)
    return pl.pallas_call(
        conv_kernel,
        out_shape=(
            jax.ShapeDtypeStruct(features.shape, jnp.bfloat16),
            jax.ShapeDtypeStruct(features.shape, jnp.bfloat16),
            jax.ShapeDtypeStruct((27, 2, channels, channels // 2), jnp.float32),
        ),
        in_specs=[pl.BlockSpec(memory_space=pltpu.SMEM)] + [vmem] * 11,
        out_specs=(vmem, vmem, vmem),
        scratch_shapes=[
            pltpu.VMEM((3 * bricks, 8, 8, 8, channels), jnp.float32),
            pltpu.VMEM((10, 10, 24, channels), jnp.float32),
            pltpu.VMEM((3, bricks, 640, 3 * channels), jnp.bfloat16),
            pltpu.VMEM((3, bricks, 640, 3 * channels), jnp.bfloat16),
            pltpu.VMEM((voxels, channels), jnp.float32),
        ],
        compiler_params=pltpu.CompilerParams(vmem_limit_bytes=VMEM_BYTES),
    )(lookup, features, active, hidden_t, *hiddens, *grads, weight, weight_t)


def scatter_kernel(scale, terms, result, r0, r1, r2, r3, r4, r5, send, recv):
    space, scene = lax.axis_index("space"), lax.axis_index("scene")
    core, x = scene % 2, scene // 2
    y, low, high = space % 2, (space // 2) % 2, space // 4
    partner = {
        "core": (space, scene + 1 - 2 * core),
        "x": (space, scene + 2 - 4 * x),
        "y": (space + 1 - 2 * y, scene),
        "low": (space + 2 - 4 * low, scene),
        "high": (space + 4 - 8 * high, scene),
    }
    barrier = pltpu.get_barrier_semaphore()
    for device in partner.values():
        pl.semaphore_signal(barrier, inc=1, device_id=device, device_id_type=MESH)
    pl.semaphore_wait(barrier, 5)

    chunks = r0.shape[0]
    copies = {}

    def begin(stage, k, source, target, axis):
        copy = pltpu.make_async_remote_copy(
            src_ref=source, dst_ref=target, send_sem=send.at[stage, k], recv_sem=recv.at[stage, k],
            device_id=partner[axis], device_id_type=MESH,
        )
        copy.start()
        copies[stage, k] = copy

    def advance(stage, k):
        taps = pl.ds(GROUP * k, GROUP)
        x_first = k % 2 == 0
        if stage == 0:
            begin(0, k, terms.at[taps, :, :, :, :, 1 - core], r0.at[k], "core")
            return
        copies[stage - 1, k].wait_recv()
        if stage == 1:
            r0[k] = r0[k] + terms[taps, :, :, :, :, core]
            if x_first:
                begin(1, k, r0.at[k, :, 1 - x], r1.at[k], "x")
            else:
                begin(1, k, r0.at[k, :, :, :, :, 1 - y], r1.at[k], "y")
        elif stage == 2:
            if x_first:
                r1[k] = r1[k] + r0[k, :, x]
                begin(2, k, r1.at[k, :, :, :, 1 - y], r2.at[k], "y")
            else:
                r1[k] = r1[k] + r0[k, :, :, :, :, y]
                begin(2, k, r1.at[k, :, 1 - x], r2.at[k], "x")
        elif stage == 3:
            r2[k] = r2[k] + (r1[k, :, :, :, y] if x_first else r1[k, :, x])
            begin(3, k, r2.at[k, :, :, 1 - low], r3.at[k], "low")
        elif stage == 4:
            r3[k] = r3[k] + r2[k, :, :, low]
            begin(4, k, r3.at[k, :, 1 - high], r4.at[k], "high")
        elif stage == 5:
            r4[k] = r4[k] + r3[k, :, high]
            begin(5, k, r4.at[k], r5.at[k], "core")
        else:
            mine, other = r4[k] * scale, r5[k] * scale
            first = jnp.where(core == 0, mine, other)
            second = jnp.where(core == 0, other, mine)
            both = jnp.concatenate([first, second], axis=1)
            half = both.shape[-1] // 2
            result[taps] = jnp.where(core == 0, both[:, :, :half], both[:, :, half:])

    ahead = 2
    for k in range(min(ahead, chunks)):
        advance(0, k)
    for at in range(chunks + 6):
        if at + ahead < chunks:
            advance(0, at + ahead)
        for stage in range(1, 7):
            k = at - (stage - 1)
            if 0 <= k < chunks:
                advance(stage, k)
    for copy in copies.values():
        copy.wait_send()


def scatter_sum(terms, scale):
    taps, _, channels, half = terms.shape
    rows = channels // 16
    chunks = taps // GROUP
    vmem = pl.BlockSpec(memory_space=pltpu.VMEM)
    f32 = jnp.float32
    tail = (rows, half)
    return pl.pallas_call(
        functools.partial(scatter_kernel, scale),
        out_shape=jax.ShapeDtypeStruct((taps, 2 * rows, half // 2), f32),
        in_specs=[vmem],
        out_specs=vmem,
        scratch_shapes=[
            pltpu.VMEM((chunks, GROUP, 2, 2, 2, 2) + tail, f32),
            pltpu.VMEM((chunks, GROUP, 2, 2, 2) + tail, f32),
            pltpu.VMEM((chunks, GROUP, 2, 2) + tail, f32),
            pltpu.VMEM((chunks, GROUP, 2) + tail, f32),
            pltpu.VMEM((chunks, GROUP) + tail, f32),
            pltpu.VMEM((chunks, GROUP) + tail, f32),
            pltpu.SemaphoreType.DMA((6, chunks)),
            pltpu.SemaphoreType.DMA((6, chunks)),
        ],
        compiler_params=pltpu.CompilerParams(
            collective_id=0, has_side_effects=True, vmem_limit_bytes=VMEM_BYTES
        ),
    )(terms.reshape(taps, 2, 2, 2, 2, 2, rows, half))


def per_device(features, cotangent, weight, counts, neighbours, occupancy):
    shape = features.shape
    bricks, extent, channels = shape[1], shape[2], shape[-1]
    voxels = extent * extent * extent
    feats = features.reshape(bricks, voxels, channels)
    slot_live = (jnp.arange(bricks, dtype=jnp.int32) < counts[0, 0]).astype(jnp.int32)
    active = (occupancy[0] * slot_live[:, None]).reshape(bricks, voxels, 1)
    live = active.astype(jnp.bfloat16)
    grad = cotangent.reshape(bricks, voxels, channels) * live
    hidden = jnp.maximum(feats, 0) * live
    grad_left, grad_right = both_sides(grad)
    hid_left, hid_right = both_sides(hidden)
    first_id = (lax.axis_index("space") - 1) * bricks
    linked = neighbours[0]
    local_ids = jnp.where(linked >= 0, linked - first_id, -1)
    centre = (bricks + jnp.arange(bricks, dtype=jnp.int32))[:, None]
    lookup = jnp.concatenate([local_ids[:, :13], centre, local_ids[:, 13:]], axis=1)
    weight_t = weight[::-1].swapaxes(1, 2).reshape(9, 3 * channels, channels)
    outputs, input_grad, terms = convolve(
        lookup, feats, active.astype(jnp.float32), hidden.swapaxes(1, 2),
        (hid_left, hidden, hid_right), (grad_left, grad, grad_right),
        weight.reshape(9, 3 * channels, channels), weight_t,
    )
    space, scene = lax.axis_size("space"), lax.axis_size("scene")
    scale = float(scene * space * bricks * voxels) ** (-0.5)
    if (space, scene) == (8, 4):
        weight_grad = scatter_sum(terms, scale)
    else:
        whole = jnp.concatenate([terms[:, 0], terms[:, 1]], axis=2) * scale
        across = lax.psum_scatter(whole, "scene", scatter_dimension=2, tiled=True)
        weight_grad = lax.psum_scatter(across, "space", scatter_dimension=1, tiled=True)
    return outputs.reshape(shape), input_grad.reshape(shape), weight_grad


def solution(mesh):
    field = P("scene", "space", None, None, None, None)
    in_specs = (field, field, P(), P("scene", "space"), P("scene", "space", None), P("scene", "space", None))
    out_specs = (field, field, P(None, "space", "scene"))
    return jax.shard_map(per_device, mesh=mesh, in_specs=in_specs, out_specs=out_specs, check_vma=False)
```

```python
import functools

import jax
import jax.numpy as jnp
from jax import lax
from jax.experimental import pallas as pl
from jax.experimental.pallas import tpu as pltpu
from jax.sharding import PartitionSpec as P

MESH = pl.DeviceIdType.MESH
VMEM_BYTES = 56 * 1024 * 1024
GROUP = 3
LAG = 2


def both_sides(cells):
    count = lax.axis_size("space")
    ends = count - 1
    left = lax.ppermute(cells, "space", [(i, i + 1) for i in range(ends)])
    right = lax.ppermute(cells, "space", [(i + 1, i) for i in range(ends)])
    return left, right


def spans(shift):
    if shift < 0:
        return slice(7, 8), slice(0, 1)
    if shift == 0:
        return slice(0, 8), slice(1, 9)
    return slice(0, 1), slice(9, 10)


def spans_z(shift):
    if shift < 0:
        return slice(7, 8), slice(7, 8)
    if shift == 0:
        return slice(0, 8), slice(8, 16)
    return slice(0, 1), slice(16, 17)


def fill_copies(lookup, bricks, sides, window, staged, copies):
    channels = staged.shape[-1]
    for side, ref in enumerate(sides):
        for b in range(bricks):

            def widen(x, carry, ref=ref, b=b, at=side * bricks + b):
                rows = ref[b, pl.ds(pl.multiple_of(x * 64, 64), 64), :]
                window[at, x] = rows.astype(jnp.float32).reshape(8, 8, channels)
                return carry

            lax.fori_loop(0, 8, widen, 0)
    for b in range(bricks):
        for sx in (-1, 0, 1):
            for sy in (-1, 0, 1):
                for sz in (-1, 0, 1):
                    (from_x, to_x), (from_y, to_y), (from_z, to_z) = spans(sx), spans(sy), spans_z(sz)
                    if sx == sy == sz == 0:
                        staged[to_x, to_y, to_z, :] = window[bricks + b, from_x, from_y, from_z, :]
                        continue
                    at = lookup[b, 9 * (sx + 1) + 3 * (sy + 1) + sz + 1]
                    inside = (at >= 0).astype(jnp.float32)
                    taken = window[jnp.maximum(at, 0), from_x, from_y, from_z, :]
                    staged[to_x, to_y, to_z, :] = taken * inside
        for y in range(3):
            for z in range(3):

                def pack(x, carry, b=b, y=y, z=z):
                    rows = staged[x, y : y + 8, 7 + z : 15 + z, :]
                    copies[y, b, pl.ds(pl.multiple_of(x * 64, 64), 64), z * channels : (z + 1) * channels] = (
                        rows.reshape(64, channels).astype(jnp.bfloat16)
                    )
                    return carry

                lax.fori_loop(0, 10, pack, 0)


def gradient_kernel(lookup, hidden_t, left, grad, right, terms, copies, window, staged):
    bricks = grad.shape[0]
    channels = grad.shape[-1]
    half = channels // 2
    fill_copies(lookup, bricks, (left, grad, right), window, staged, copies)

    def gradient(i, carry):
        for z in range(3):
            summed = None
            for b in range(bricks):
                start = pl.multiple_of((i // 3) * 64, 64)
                rows = copies[i % 3, b, pl.ds(start, 512), z * channels : (z + 1) * channels]
                product = jnp.dot(hidden_t[b], rows, preferred_element_type=jnp.float32)
                summed = product if summed is None else summed + product
            tap = 26 - 3 * i - z
            terms[tap, 0] = summed[:, :half]
            terms[tap, 1] = summed[:, half:]
        return carry

    lax.fori_loop(0, 9, gradient, 0)


def blocks_kernel(lookup, left, hidden, right, copies, window, staged):
    fill_copies(lookup, hidden.shape[0], (left, hidden, right), window, staged, copies)


def vmem_specs(count):
    return [pl.BlockSpec(memory_space=pltpu.VMEM)] * count


def block_scratch(bricks, channels):
    return [
        pltpu.VMEM((3 * bricks, 8, 8, 8, channels), jnp.float32),
        pltpu.VMEM((10, 10, 24, channels), jnp.float32),
    ]


def gradient_terms(lookup, hidden_t, grads):
    bricks, voxels, channels = grads[1].shape
    return pl.pallas_call(
        gradient_kernel,
        out_shape=(
            jax.ShapeDtypeStruct((27, 2, channels, channels // 2), jnp.float32),
            jax.ShapeDtypeStruct((3, bricks, 640, 3 * channels), jnp.bfloat16),
        ),
        in_specs=[pl.BlockSpec(memory_space=pltpu.SMEM)] + vmem_specs(4),
        out_specs=tuple(vmem_specs(2)),
        scratch_shapes=block_scratch(bricks, channels),
        compiler_params=pltpu.CompilerParams(vmem_limit_bytes=VMEM_BYTES),
        cost_estimate=pl.CostEstimate(
            flops=2 * 27 * bricks * voxels * channels * channels, bytes_accessed=60_000_000, transcendentals=0
        ),
    )(lookup, hidden_t, *grads)


def halo_blocks(lookup, hiddens):
    bricks, voxels, channels = hiddens[1].shape
    return pl.pallas_call(
        blocks_kernel,
        out_shape=jax.ShapeDtypeStruct((3, bricks, 640, 3 * channels), jnp.bfloat16),
        in_specs=[pl.BlockSpec(memory_space=pltpu.SMEM)] + vmem_specs(3),
        out_specs=vmem_specs(1)[0],
        scratch_shapes=block_scratch(bricks, channels),
        compiler_params=pltpu.CompilerParams(vmem_limit_bytes=VMEM_BYTES),
        cost_estimate=pl.CostEstimate(flops=0, bytes_accessed=30_000_000, transcendentals=0),
    )(lookup, *hiddens)


def scatter_kernel(
    scale, terms, features, active, hidden, grad, hid_source, weight_source, grad_source, weight_t_source,
    outputs, input_grad, result,
    hid_copies, weight, grad_copies, weight_t, total,
    r0, r1, r2, r3, r4, r5, local, send, recv,
):
    space, scene = lax.axis_index("space"), lax.axis_index("scene")
    core, x = scene % 2, scene // 2
    y, low, high = space % 2, (space // 2) % 2, space // 4
    partner = {
        "core": (space, scene + 1 - 2 * core),
        "x": (space, scene + 2 - 4 * x),
        "y": (space + 1 - 2 * y, scene),
        "low": (space + 2 - 4 * low, scene),
        "high": (space + 4 - 8 * high, scene),
    }
    barrier = pltpu.get_barrier_semaphore()
    for device in partner.values():
        pl.semaphore_signal(barrier, inc=1, device_id=device, device_id_type=MESH)
    pl.semaphore_wait(barrier, 5)

    moves = []
    for n, (source, target) in enumerate(
        ((hid_source, hid_copies), (weight_source, weight), (grad_source, grad_copies), (weight_t_source, weight_t))
    ):
        moves.append(pltpu.make_async_copy(source, target, local.at[n]))
        moves[n].start()

    def convolve(n):
        task, part = n // 3, n % 3
        forward, b = task < bricks, task % bricks
        copied, matrix = (hid_copies, weight) if forward else (grad_copies, weight_t)
        if part == 0:
            if b == 0:
                for move in moves[:2] if forward else moves[2:]:
                    move.wait()
            total[...] = jnp.zeros_like(total)

        def step(i, carry):
            rows = copied[i % 3, b, pl.ds(pl.multiple_of((i // 3) * 64, 64), 512), :]
            total[...] += jnp.dot(rows, matrix[i], preferred_element_type=jnp.float32)
            return carry

        lax.fori_loop(3 * part, 3 * part + 3, step, 0)
        if part == 2 and forward:
            summed = (features[b].astype(jnp.float32) + total[...]) * active[b]
            outputs[b] = summed.astype(jnp.bfloat16)
        elif part == 2:
            kept = jnp.where(hidden[b].astype(jnp.float32) > 0, total[...], 0.0)
            input_grad[b] = (grad[b].astype(jnp.float32) + kept).astype(jnp.bfloat16)

    bricks = features.shape[0]
    chunks = r0.shape[0]
    copies = {}

    def begin(stage, k, source, target, axis):
        copy = pltpu.make_async_remote_copy(
            src_ref=source, dst_ref=target, send_sem=send.at[stage, k], recv_sem=recv.at[stage, k],
            device_id=partner[axis], device_id_type=MESH,
        )
        copy.start()
        copies[stage, k] = copy

    def advance(stage, k):
        taps = pl.ds(GROUP * k, GROUP)
        x_first = k % 2 == 0
        if stage == 0:
            begin(0, k, terms.at[taps, :, :, :, :, 1 - core], r0.at[k], "core")
            return
        copies[stage - 1, k].wait_recv()
        if stage == 1:
            r0[k] = r0[k] + terms[taps, :, :, :, :, core]
            if x_first:
                begin(1, k, r0.at[k, :, 1 - x], r1.at[k], "x")
            else:
                begin(1, k, r0.at[k, :, :, :, :, 1 - y], r1.at[k], "y")
        elif stage == 2:
            if x_first:
                r1[k] = r1[k] + r0[k, :, x]
                begin(2, k, r1.at[k, :, :, :, 1 - y], r2.at[k], "y")
            else:
                r1[k] = r1[k] + r0[k, :, :, :, :, y]
                begin(2, k, r1.at[k, :, 1 - x], r2.at[k], "x")
        elif stage == 3:
            r2[k] = r2[k] + (r1[k, :, :, :, y] if x_first else r1[k, :, x])
            begin(3, k, r2.at[k, :, :, 1 - low], r3.at[k], "low")
        elif stage == 4:
            r3[k] = r3[k] + r2[k, :, :, low]
            begin(4, k, r3.at[k, :, 1 - high], r4.at[k], "high")
        elif stage == 5:
            r4[k] = r4[k] + r3[k, :, high]
            begin(5, k, r4.at[k], r5.at[k], "core")
        else:
            mine, other = r4[k] * scale, r5[k] * scale
            first = jnp.where(core == 0, mine, other)
            second = jnp.where(core == 0, other, mine)
            both = jnp.concatenate([first, second], axis=1)
            half = both.shape[-1] // 2
            result[taps] = jnp.where(core == 0, both[:, :, :half], both[:, :, half:])

    ahead = 2
    for k in range(min(ahead, chunks)):
        advance(0, k)
    parts = 6 * bricks
    for at in range(chunks + 5 * LAG):
        if at + ahead < chunks:
            advance(0, at + ahead)
        for stage in range(1, 7):
            k = at - LAG * (stage - 1)
            if 0 <= k < chunks:
                advance(stage, k)
        if 1 <= at <= parts:
            convolve(at - 1)
    for n in range(chunks + 5 * LAG - 1, parts):
        convolve(n)
    for copy in copies.values():
        copy.wait_send()


def scatter_sum(terms, scale, fields, streamed):
    taps, _, channels, half = terms.shape
    features = fields[0]
    rows = channels // 16
    chunks = taps // GROUP
    f32 = jnp.float32
    tail = (rows, half)
    return pl.pallas_call(
        functools.partial(scatter_kernel, scale),
        out_shape=(
            jax.ShapeDtypeStruct(features.shape, jnp.bfloat16),
            jax.ShapeDtypeStruct(features.shape, jnp.bfloat16),
            jax.ShapeDtypeStruct((taps, 2 * rows, half // 2), f32),
        ),
        in_specs=vmem_specs(5) + [pl.BlockSpec(memory_space=pl.ANY)] * 4,
        out_specs=tuple(vmem_specs(3)),
        scratch_shapes=[pltpu.VMEM(array.shape, array.dtype) for array in streamed]
        + [
            pltpu.VMEM(features.shape[1:], f32),
            pltpu.VMEM((chunks, GROUP, 2, 2, 2, 2) + tail, f32),
            pltpu.VMEM((chunks, GROUP, 2, 2, 2) + tail, f32),
            pltpu.VMEM((chunks, GROUP, 2, 2) + tail, f32),
            pltpu.VMEM((chunks, GROUP, 2) + tail, f32),
            pltpu.VMEM((chunks, GROUP) + tail, f32),
            pltpu.VMEM((chunks, GROUP) + tail, f32),
            pltpu.SemaphoreType.DMA((4,)),
            pltpu.SemaphoreType.DMA((6, chunks)),
            pltpu.SemaphoreType.DMA((6, chunks)),
        ],
        compiler_params=pltpu.CompilerParams(
            collective_id=0, has_side_effects=True, vmem_limit_bytes=VMEM_BYTES
        ),
    )(terms.reshape(taps, 2, 2, 2, 2, 2, rows, half), *fields, *streamed)


def conv_kernel(features, active, hidden, grad, hid_copies, grad_copies, weight, weight_t, outputs, input_grad, total):
    for b in range(features.shape[0]):
        for copied, matrix in ((hid_copies, weight), (grad_copies, weight_t)):
            total[...] = jnp.zeros_like(total)

            def step(i, carry, b=b, copied=copied, matrix=matrix):
                rows = copied[i % 3, b, pl.ds(pl.multiple_of((i // 3) * 64, 64), 512), :]
                total[...] += jnp.dot(rows, matrix[i], preferred_element_type=jnp.float32)
                return carry

            lax.fori_loop(0, 9, step, 0)
            if copied is hid_copies:
                summed = (features[b].astype(jnp.float32) + total[...]) * active[b]
                outputs[b] = summed.astype(jnp.bfloat16)
            else:
                kept = jnp.where(hidden[b].astype(jnp.float32) > 0, total[...], 0.0)
                input_grad[b] = (grad[b].astype(jnp.float32) + kept).astype(jnp.bfloat16)


def convolve_alone(fields, streamed):
    shape = jax.ShapeDtypeStruct(fields[0].shape, jnp.bfloat16)
    hid_copies, weight, grad_copies, weight_t = streamed
    return pl.pallas_call(
        conv_kernel,
        out_shape=(shape, shape),
        in_specs=vmem_specs(8),
        out_specs=tuple(vmem_specs(2)),
        scratch_shapes=[pltpu.VMEM(fields[0].shape[1:], jnp.float32)],
        compiler_params=pltpu.CompilerParams(vmem_limit_bytes=VMEM_BYTES),
    )(*fields, hid_copies, grad_copies, weight, weight_t)


def per_device(features, cotangent, weight, counts, neighbours, occupancy):
    shape = features.shape
    bricks, extent, channels = shape[1], shape[2], shape[-1]
    voxels = extent * extent * extent
    feats = features.reshape(bricks, voxels, channels)
    slot_live = (jnp.arange(bricks, dtype=jnp.int32) < counts[0, 0]).astype(jnp.int32)
    active = (occupancy[0] * slot_live[:, None]).reshape(bricks, voxels, 1)
    live = active.astype(jnp.bfloat16)
    grad = cotangent.reshape(bricks, voxels, channels) * live
    hidden = jnp.maximum(feats, 0) * live
    grad_left, grad_right = both_sides(grad)
    hid_left, hid_right = both_sides(hidden)
    first_id = (lax.axis_index("space") - 1) * bricks
    linked = neighbours[0]
    local_ids = jnp.where(linked >= 0, linked - first_id, -1)
    centre = (bricks + jnp.arange(bricks, dtype=jnp.int32))[:, None]
    lookup = jnp.concatenate([local_ids[:, :13], centre, local_ids[:, 13:]], axis=1)
    weight_t = weight[::-1].swapaxes(1, 2).reshape(9, 3 * channels, channels)
    terms, grad_copies = gradient_terms(lookup, hidden.swapaxes(1, 2), (grad_left, grad, grad_right))
    hid_copies = halo_blocks(lookup, (hid_left, hidden, hid_right))
    fields = (feats, active.astype(jnp.float32), hidden, grad)
    streamed = (hid_copies, weight.reshape(9, 3 * channels, channels), grad_copies, weight_t)
    space, scene = lax.axis_size("space"), lax.axis_size("scene")
    scale = float(scene * space * bricks * voxels) ** (-0.5)
    if (space, scene) == (8, 4):
        outputs, input_grad, weight_grad = scatter_sum(terms, scale, fields, streamed)
    else:
        outputs, input_grad = convolve_alone(fields, streamed)
        whole = jnp.concatenate([terms[:, 0], terms[:, 1]], axis=2) * scale
        across = lax.psum_scatter(whole, "scene", scatter_dimension=2, tiled=True)
        weight_grad = lax.psum_scatter(across, "space", scatter_dimension=1, tiled=True)
    return outputs.reshape(shape), input_grad.reshape(shape), weight_grad


def solution(mesh):
    field = P("scene", "space", None, None, None, None)
    in_specs = (field, field, P(), P("scene", "space"), P("scene", "space", None), P("scene", "space", None))
    out_specs = (field, field, P(None, "space", "scene"))
    return jax.shard_map(per_device, mesh=mesh, in_specs=in_specs, out_specs=out_specs, check_vma=False)
```

```python
import functools

import jax
import jax.numpy as jnp
from jax import lax
from jax.experimental import pallas as pl
from jax.experimental.pallas import tpu as pltpu
from jax.sharding import PartitionSpec as P

MESH = pl.DeviceIdType.MESH
VMEM_BYTES = 56 * 1024 * 1024
GROUP = 3
LAG = 2


def both_sides(cells):
    count = lax.axis_size("space")
    ends = count - 1
    left = lax.ppermute(cells, "space", [(i, i + 1) for i in range(ends)])
    right = lax.ppermute(cells, "space", [(i + 1, i) for i in range(ends)])
    return left, right


def spans(shift):
    if shift < 0:
        return slice(7, 8), slice(0, 1)
    if shift == 0:
        return slice(0, 8), slice(1, 9)
    return slice(0, 1), slice(9, 10)


def spans_z(shift):
    if shift < 0:
        return slice(7, 8), slice(7, 8)
    if shift == 0:
        return slice(0, 8), slice(8, 16)
    return slice(0, 1), slice(16, 17)


def prepare_kernel(features, cotangent, active, hidden, grad, packed_hidden, packed_grad, block):
    channels = block.shape[-1]
    for b in range(features.shape[0]):
        for source, target, packed in ((cotangent, grad, packed_grad), (features, hidden, packed_hidden)):

            def mask(x, carry, source=source, target=target, b=b):
                at = pl.ds(pl.multiple_of(x * 64, 64), 64)
                rows = source[b, at, :].astype(jnp.float32)
                if source is features:
                    rows = jnp.maximum(rows, 0)
                rows = rows * active[b, at, :]
                target[b, at, :] = rows.astype(jnp.bfloat16)
                block[x] = rows.reshape(8, 8, channels)
                return carry

            lax.fori_loop(0, 8, mask, 0)
            for n, x in enumerate((0, 7)):
                packed[b, 64 * n : 64 * n + 64, :] = block[x].reshape(64, channels).astype(jnp.bfloat16)
            for x in range(1, 7):
                faces_y = jnp.concatenate([block[x, 0], block[x, 7]], axis=0)
                packed[b, 112 + 16 * x : 128 + 16 * x, :] = faces_y.astype(jnp.bfloat16)
                faces_z = jnp.concatenate([block[x, :, 0, :], block[x, :, 7, :]], axis=0)
                packed[b, 208 + 16 * x : 224 + 16 * x, :] = faces_z.astype(jnp.bfloat16)


def prepare(features, cotangent, active):
    bricks, _, channels = features.shape
    whole = jax.ShapeDtypeStruct(features.shape, jnp.bfloat16)
    surface = jax.ShapeDtypeStruct((bricks, 320, channels), jnp.bfloat16)
    return pl.pallas_call(
        prepare_kernel,
        out_shape=(whole, whole, surface, surface),
        in_specs=vmem_specs(3),
        out_specs=tuple(vmem_specs(4)),
        scratch_shapes=[pltpu.VMEM((8, 8, 8, channels), jnp.float32)],
        compiler_params=pltpu.CompilerParams(vmem_limit_bytes=VMEM_BYTES),
    )(features, cotangent, active)


def unpack(packed, b, at, window):
    channels = window.shape[-1]
    for n, x in enumerate((0, 7)):
        rows = packed[b, 64 * n : 64 * n + 64, :].astype(jnp.float32)
        window[at, x] = rows.reshape(8, 8, channels)
    for x in range(1, 7):
        faces_y = packed[b, 112 + 16 * x : 128 + 16 * x, :].astype(jnp.float32)
        faces_z = packed[b, 208 + 16 * x : 224 + 16 * x, :].astype(jnp.float32)
        window[at, x, 0], window[at, x, 7] = faces_y[:8], faces_y[8:]
        window[at, x, :, 0, :], window[at, x, :, 7, :] = faces_z[:8], faces_z[8:]


def fill_copies(lookup, bricks, sides, window, staged, copies):
    channels = staged.shape[-1]
    left, own, right = sides
    for b in range(bricks):
        unpack(left, b, b, window)
        unpack(right, b, 2 * bricks + b, window)

        def widen(x, carry, b=b):
            rows = own[b, pl.ds(pl.multiple_of(x * 64, 64), 64), :]
            window[bricks + b, x] = rows.astype(jnp.float32).reshape(8, 8, channels)
            return carry

        lax.fori_loop(0, 8, widen, 0)
    for b in range(bricks):
        for sx in (-1, 0, 1):
            for sy in (-1, 0, 1):
                for sz in (-1, 0, 1):
                    (from_x, to_x), (from_y, to_y), (from_z, to_z) = spans(sx), spans(sy), spans_z(sz)
                    if sx == sy == sz == 0:
                        staged[to_x, to_y, to_z, :] = window[bricks + b, from_x, from_y, from_z, :]
                        continue
                    at = lookup[b, 9 * (sx + 1) + 3 * (sy + 1) + sz + 1]
                    inside = (at >= 0).astype(jnp.float32)
                    taken = window[jnp.maximum(at, 0), from_x, from_y, from_z, :]
                    staged[to_x, to_y, to_z, :] = taken * inside
        for y in range(3):
            for z in range(3):

                def pack(x, carry, b=b, y=y, z=z):
                    rows = staged[x, y : y + 8, 7 + z : 15 + z, :]
                    copies[y, b, pl.ds(pl.multiple_of(x * 64, 64), 64), z * channels : (z + 1) * channels] = (
                        rows.reshape(64, channels).astype(jnp.bfloat16)
                    )
                    return carry

                lax.fori_loop(0, 10, pack, 0)


def gradient_kernel(lookup, hidden_t, left, grad, right, terms, copies, window, staged):
    bricks = grad.shape[0]
    channels = grad.shape[-1]
    half = channels // 2
    fill_copies(lookup, bricks, (left, grad, right), window, staged, copies)

    def gradient(i, carry):
        for z in range(3):
            summed = None
            for b in range(bricks):
                start = pl.multiple_of((i // 3) * 64, 64)
                rows = copies[i % 3, b, pl.ds(start, 512), z * channels : (z + 1) * channels]
                product = jnp.dot(hidden_t[b], rows, preferred_element_type=jnp.float32)
                summed = product if summed is None else summed + product
            tap = 26 - 3 * i - z
            terms[tap, 0] = summed[:, :half]
            terms[tap, 1] = summed[:, half:]
        return carry

    lax.fori_loop(0, 9, gradient, 0)


def blocks_kernel(lookup, left, hidden, right, copies, window, staged):
    fill_copies(lookup, hidden.shape[0], (left, hidden, right), window, staged, copies)


def vmem_specs(count):
    return [pl.BlockSpec(memory_space=pltpu.VMEM)] * count


def block_scratch(bricks, channels):
    return [
        pltpu.VMEM((3 * bricks, 8, 8, 8, channels), jnp.float32),
        pltpu.VMEM((10, 10, 24, channels), jnp.float32),
    ]


def gradient_terms(lookup, hidden_t, grads):
    bricks, voxels, channels = grads[1].shape
    return pl.pallas_call(
        gradient_kernel,
        out_shape=(
            jax.ShapeDtypeStruct((27, 2, channels, channels // 2), jnp.float32),
            jax.ShapeDtypeStruct((3, bricks, 640, 3 * channels), jnp.bfloat16),
        ),
        in_specs=[pl.BlockSpec(memory_space=pltpu.SMEM)] + vmem_specs(4),
        out_specs=tuple(vmem_specs(2)),
        scratch_shapes=block_scratch(bricks, channels),
        compiler_params=pltpu.CompilerParams(vmem_limit_bytes=VMEM_BYTES),
        cost_estimate=pl.CostEstimate(
            flops=2 * 27 * bricks * voxels * channels * channels, bytes_accessed=60_000_000, transcendentals=0
        ),
    )(lookup, hidden_t, *grads)


def halo_blocks(lookup, hiddens):
    bricks, voxels, channels = hiddens[1].shape
    return pl.pallas_call(
        blocks_kernel,
        out_shape=jax.ShapeDtypeStruct((3, bricks, 640, 3 * channels), jnp.bfloat16),
        in_specs=[pl.BlockSpec(memory_space=pltpu.SMEM)] + vmem_specs(3),
        out_specs=vmem_specs(1)[0],
        scratch_shapes=block_scratch(bricks, channels),
        compiler_params=pltpu.CompilerParams(vmem_limit_bytes=VMEM_BYTES),
        cost_estimate=pl.CostEstimate(flops=0, bytes_accessed=30_000_000, transcendentals=0),
    )(lookup, *hiddens)


def scatter_kernel(
    scale, terms, features, active, hidden, grad, hid_source, weight_source, grad_source, weight_t_source,
    outputs, input_grad, result,
    hid_copies, weight, grad_copies, weight_t, total,
    r0, r1, r2, r3, r4, r5, local, send, recv,
):
    space, scene = lax.axis_index("space"), lax.axis_index("scene")
    core, x = scene % 2, scene // 2
    y, low, high = space % 2, (space // 2) % 2, space // 4
    partner = {
        "core": (space, scene + 1 - 2 * core),
        "x": (space, scene + 2 - 4 * x),
        "y": (space + 1 - 2 * y, scene),
        "low": (space + 2 - 4 * low, scene),
        "high": (space + 4 - 8 * high, scene),
    }
    barrier = pltpu.get_barrier_semaphore()
    for device in partner.values():
        pl.semaphore_signal(barrier, inc=1, device_id=device, device_id_type=MESH)
    pl.semaphore_wait(barrier, 5)

    moves = []
    for n, (source, target) in enumerate(
        ((hid_source, hid_copies), (weight_source, weight), (grad_source, grad_copies), (weight_t_source, weight_t))
    ):
        moves.append(pltpu.make_async_copy(source, target, local.at[n]))
        moves[n].start()

    def convolve(n):
        task, part = n // 3, n % 3
        forward, b = task < bricks, task % bricks
        copied, matrix = (hid_copies, weight) if forward else (grad_copies, weight_t)
        if part == 0:
            if b == 0:
                for move in moves[:2] if forward else moves[2:]:
                    move.wait()
            total[...] = jnp.zeros_like(total)

        def step(i, carry):
            rows = copied[i % 3, b, pl.ds(pl.multiple_of((i // 3) * 64, 64), 512), :]
            total[...] += jnp.dot(rows, matrix[i], preferred_element_type=jnp.float32)
            return carry

        lax.fori_loop(3 * part, 3 * part + 3, step, 0)
        if part == 2 and forward:
            summed = (features[b].astype(jnp.float32) + total[...]) * active[b]
            outputs[b] = summed.astype(jnp.bfloat16)
        elif part == 2:
            kept = jnp.where(hidden[b].astype(jnp.float32) > 0, total[...], 0.0)
            input_grad[b] = (grad[b].astype(jnp.float32) + kept).astype(jnp.bfloat16)

    bricks = features.shape[0]
    chunks = r0.shape[0]
    copies = {}

    def begin(stage, k, source, target, axis):
        copy = pltpu.make_async_remote_copy(
            src_ref=source, dst_ref=target, send_sem=send.at[stage, k], recv_sem=recv.at[stage, k],
            device_id=partner[axis], device_id_type=MESH,
        )
        copy.start()
        copies[stage, k] = copy

    def advance(stage, k):
        taps = pl.ds(GROUP * k, GROUP)
        x_first = k % 2 == 0
        if stage == 0:
            begin(0, k, terms.at[taps, :, :, :, :, 1 - core], r0.at[k], "core")
            return
        copies[stage - 1, k].wait_recv()
        if stage == 1:
            r0[k] = r0[k] + terms[taps, :, :, :, :, core]
            if x_first:
                begin(1, k, r0.at[k, :, 1 - x], r1.at[k], "x")
            else:
                begin(1, k, r0.at[k, :, :, :, :, 1 - y], r1.at[k], "y")
        elif stage == 2:
            if x_first:
                r1[k] = r1[k] + r0[k, :, x]
                begin(2, k, r1.at[k, :, :, :, 1 - y], r2.at[k], "y")
            else:
                r1[k] = r1[k] + r0[k, :, :, :, :, y]
                begin(2, k, r1.at[k, :, 1 - x], r2.at[k], "x")
        elif stage == 3:
            r2[k] = r2[k] + (r1[k, :, :, :, y] if x_first else r1[k, :, x])
            begin(3, k, r2.at[k, :, :, 1 - low], r3.at[k], "low")
        elif stage == 4:
            r3[k] = r3[k] + r2[k, :, :, low]
            begin(4, k, r3.at[k, :, 1 - high], r4.at[k], "high")
        elif stage == 5:
            r4[k] = r4[k] + r3[k, :, high]
            begin(5, k, r4.at[k], r5.at[k], "core")
        else:
            mine, other = r4[k] * scale, r5[k] * scale
            first = jnp.where(core == 0, mine, other)
            second = jnp.where(core == 0, other, mine)
            both = jnp.concatenate([first, second], axis=1)
            half = both.shape[-1] // 2
            result[taps] = jnp.where(core == 0, both[:, :, :half], both[:, :, half:])

    ahead = 2
    for k in range(min(ahead, chunks)):
        advance(0, k)
    parts = 6 * bricks
    for at in range(chunks + 5 * LAG):
        if at + ahead < chunks:
            advance(0, at + ahead)
        for stage in range(1, 7):
            k = at - LAG * (stage - 1)
            if 0 <= k < chunks:
                advance(stage, k)
        if 1 <= at <= parts:
            convolve(at - 1)
    for n in range(chunks + 5 * LAG - 1, parts):
        convolve(n)
    for copy in copies.values():
        copy.wait_send()


def scatter_sum(terms, scale, fields, streamed):
    taps, _, channels, half = terms.shape
    features = fields[0]
    rows = channels // 16
    chunks = taps // GROUP
    f32 = jnp.float32
    tail = (rows, half)
    return pl.pallas_call(
        functools.partial(scatter_kernel, scale),
        out_shape=(
            jax.ShapeDtypeStruct(features.shape, jnp.bfloat16),
            jax.ShapeDtypeStruct(features.shape, jnp.bfloat16),
            jax.ShapeDtypeStruct((taps, 2 * rows, half // 2), f32),
        ),
        in_specs=vmem_specs(5) + [pl.BlockSpec(memory_space=pl.ANY)] * 4,
        out_specs=tuple(vmem_specs(3)),
        scratch_shapes=[pltpu.VMEM(array.shape, array.dtype) for array in streamed]
        + [
            pltpu.VMEM(features.shape[1:], f32),
            pltpu.VMEM((chunks, GROUP, 2, 2, 2, 2) + tail, f32),
            pltpu.VMEM((chunks, GROUP, 2, 2, 2) + tail, f32),
            pltpu.VMEM((chunks, GROUP, 2, 2) + tail, f32),
            pltpu.VMEM((chunks, GROUP, 2) + tail, f32),
            pltpu.VMEM((chunks, GROUP) + tail, f32),
            pltpu.VMEM((chunks, GROUP) + tail, f32),
            pltpu.SemaphoreType.DMA((4,)),
            pltpu.SemaphoreType.DMA((6, chunks)),
            pltpu.SemaphoreType.DMA((6, chunks)),
        ],
        compiler_params=pltpu.CompilerParams(
            collective_id=0, has_side_effects=True, vmem_limit_bytes=VMEM_BYTES
        ),
    )(terms.reshape(taps, 2, 2, 2, 2, 2, rows, half), *fields, *streamed)


def conv_kernel(features, active, hidden, grad, hid_copies, grad_copies, weight, weight_t, outputs, input_grad, total):
    for b in range(features.shape[0]):
        for copied, matrix in ((hid_copies, weight), (grad_copies, weight_t)):
            total[...] = jnp.zeros_like(total)

            def step(i, carry, b=b, copied=copied, matrix=matrix):
                rows = copied[i % 3, b, pl.ds(pl.multiple_of((i // 3) * 64, 64), 512), :]
                total[...] += jnp.dot(rows, matrix[i], preferred_element_type=jnp.float32)
                return carry

            lax.fori_loop(0, 9, step, 0)
            if copied is hid_copies:
                summed = (features[b].astype(jnp.float32) + total[...]) * active[b]
                outputs[b] = summed.astype(jnp.bfloat16)
            else:
                kept = jnp.where(hidden[b].astype(jnp.float32) > 0, total[...], 0.0)
                input_grad[b] = (grad[b].astype(jnp.float32) + kept).astype(jnp.bfloat16)


def convolve_alone(fields, streamed):
    shape = jax.ShapeDtypeStruct(fields[0].shape, jnp.bfloat16)
    hid_copies, weight, grad_copies, weight_t = streamed
    return pl.pallas_call(
        conv_kernel,
        out_shape=(shape, shape),
        in_specs=vmem_specs(8),
        out_specs=tuple(vmem_specs(2)),
        scratch_shapes=[pltpu.VMEM(fields[0].shape[1:], jnp.float32)],
        compiler_params=pltpu.CompilerParams(vmem_limit_bytes=VMEM_BYTES),
    )(*fields, hid_copies, grad_copies, weight, weight_t)


def per_device(features, cotangent, weight, counts, neighbours, occupancy):
    shape = features.shape
    bricks, extent, channels = shape[1], shape[2], shape[-1]
    voxels = extent * extent * extent
    feats = features.reshape(bricks, voxels, channels)
    slot_live = (jnp.arange(bricks, dtype=jnp.int32) < counts[0, 0]).astype(jnp.int32)
    active = (occupancy[0] * slot_live[:, None]).reshape(bricks, voxels, 1)
    live = active.astype(jnp.float32)
    hidden, grad, packed_hidden, packed_grad = prepare(
        feats, cotangent.reshape(bricks, voxels, channels), live
    )
    grad_left, grad_right = both_sides(packed_grad)
    hid_left, hid_right = both_sides(packed_hidden)
    first_id = (lax.axis_index("space") - 1) * bricks
    linked = neighbours[0]
    local_ids = jnp.where(linked >= 0, linked - first_id, -1)
    centre = (bricks + jnp.arange(bricks, dtype=jnp.int32))[:, None]
    lookup = jnp.concatenate([local_ids[:, :13], centre, local_ids[:, 13:]], axis=1)
    weight_t = weight[::-1].swapaxes(1, 2).reshape(9, 3 * channels, channels)
    terms, grad_copies = gradient_terms(lookup, hidden.swapaxes(1, 2), (grad_left, grad, grad_right))
    hid_copies = halo_blocks(lookup, (hid_left, hidden, hid_right))
    fields = (feats, live, hidden, grad)
    streamed = (hid_copies, weight.reshape(9, 3 * channels, channels), grad_copies, weight_t)
    space, scene = lax.axis_size("space"), lax.axis_size("scene")
    scale = float(scene * space * bricks * voxels) ** (-0.5)
    if (space, scene) == (8, 4):
        outputs, input_grad, weight_grad = scatter_sum(terms, scale, fields, streamed)
    else:
        outputs, input_grad = convolve_alone(fields, streamed)
        whole = jnp.concatenate([terms[:, 0], terms[:, 1]], axis=2) * scale
        across = lax.psum_scatter(whole, "scene", scatter_dimension=2, tiled=True)
        weight_grad = lax.psum_scatter(across, "space", scatter_dimension=1, tiled=True)
    return outputs.reshape(shape), input_grad.reshape(shape), weight_grad


def solution(mesh):
    field = P("scene", "space", None, None, None, None)
    in_specs = (field, field, P(), P("scene", "space"), P("scene", "space", None), P("scene", "space", None))
    out_specs = (field, field, P(None, "space", "scene"))
    return jax.shard_map(per_device, mesh=mesh, in_specs=in_specs, out_specs=out_specs, check_vma=False)
```

```python
import functools

import jax
import jax.numpy as jnp
from jax import lax
from jax.experimental import pallas as pl
from jax.experimental.pallas import tpu as pltpu
from jax.sharding import PartitionSpec as P

MESH = pl.DeviceIdType.MESH
VMEM_BYTES = 56 * 1024 * 1024
GROUP = 3
LAG = 2
DELAY = 3


def both_sides(cells):
    count = lax.axis_size("space")
    ends = count - 1
    left = lax.ppermute(cells, "space", [(i, i + 1) for i in range(ends)])
    right = lax.ppermute(cells, "space", [(i + 1, i) for i in range(ends)])
    return left, right


def spans(shift):
    if shift < 0:
        return slice(7, 8), slice(0, 1)
    if shift == 0:
        return slice(0, 8), slice(1, 9)
    return slice(0, 1), slice(9, 10)


def spans_z(shift):
    if shift < 0:
        return slice(7, 8), slice(7, 8)
    if shift == 0:
        return slice(0, 8), slice(8, 16)
    return slice(0, 1), slice(16, 17)


def prepare_kernel(features, cotangent, active, hidden, grad, packed, block):
    channels = block.shape[-1]
    bricks = features.shape[0]
    for b in range(bricks):
        for source, target, to in ((features, hidden, b), (cotangent, grad, bricks + b)):

            def mask(x, carry, source=source, target=target, b=b):
                at = pl.ds(pl.multiple_of(x * 64, 64), 64)
                rows = source[b, at, :].astype(jnp.float32)
                if source is features:
                    rows = jnp.maximum(rows, 0)
                rows = rows * active[b, at, :]
                target[b, at, :] = rows.astype(jnp.bfloat16)
                block[x] = rows.reshape(8, 8, channels)
                return carry

            lax.fori_loop(0, 8, mask, 0)
            for n, x in enumerate((0, 7)):
                packed[to, 64 * n : 64 * n + 64, :] = block[x].reshape(64, channels).astype(jnp.bfloat16)
            for x in range(1, 7):
                faces_y = jnp.concatenate([block[x, 0], block[x, 7]], axis=0)
                packed[to, 112 + 16 * x : 128 + 16 * x, :] = faces_y.astype(jnp.bfloat16)
                faces_z = jnp.concatenate([block[x, :, 0, :], block[x, :, 7, :]], axis=0)
                packed[to, 208 + 16 * x : 224 + 16 * x, :] = faces_z.astype(jnp.bfloat16)


def prepare(features, cotangent, active):
    bricks, _, channels = features.shape
    whole = jax.ShapeDtypeStruct(features.shape, jnp.bfloat16)
    surface = jax.ShapeDtypeStruct((2 * bricks, 320, channels), jnp.bfloat16)
    return pl.pallas_call(
        prepare_kernel,
        out_shape=(whole, whole, surface),
        in_specs=vmem_specs(3),
        out_specs=tuple(vmem_specs(3)),
        scratch_shapes=[pltpu.VMEM((8, 8, 8, channels), jnp.float32)],
        compiler_params=pltpu.CompilerParams(vmem_limit_bytes=VMEM_BYTES),
    )(features, cotangent, active)


def unpack(packed, b, at, window):
    channels = window.shape[-1]
    for n, x in enumerate((0, 7)):
        rows = packed[b, 64 * n : 64 * n + 64, :].astype(jnp.float32)
        window[at, x] = rows.reshape(8, 8, channels)
    for x in range(1, 7):
        faces_y = packed[b, 112 + 16 * x : 128 + 16 * x, :].astype(jnp.float32)
        faces_z = packed[b, 208 + 16 * x : 224 + 16 * x, :].astype(jnp.float32)
        window[at, x, 0], window[at, x, 7] = faces_y[:8], faces_y[8:]
        window[at, x, :, 0, :], window[at, x, :, 7, :] = faces_z[:8], faces_z[8:]


def fill_copies(lookup, bricks, first, sides, window, staged, copies):
    channels = staged.shape[-1]
    left, own, right = sides
    for b in range(bricks):
        unpack(left, first + b, b, window)
        unpack(right, first + b, 2 * bricks + b, window)

        def widen(x, carry, b=b):
            rows = own[b, pl.ds(pl.multiple_of(x * 64, 64), 64), :]
            window[bricks + b, x] = rows.astype(jnp.float32).reshape(8, 8, channels)
            return carry

        lax.fori_loop(0, 8, widen, 0)
    for b in range(bricks):
        for sx in (-1, 0, 1):
            for sy in (-1, 0, 1):
                for sz in (-1, 0, 1):
                    (from_x, to_x), (from_y, to_y), (from_z, to_z) = spans(sx), spans(sy), spans_z(sz)
                    if sx == sy == sz == 0:
                        staged[to_x, to_y, to_z, :] = window[bricks + b, from_x, from_y, from_z, :]
                        continue
                    at = lookup[b, 9 * (sx + 1) + 3 * (sy + 1) + sz + 1]
                    inside = (at >= 0).astype(jnp.float32)
                    taken = window[jnp.maximum(at, 0), from_x, from_y, from_z, :]
                    staged[to_x, to_y, to_z, :] = taken * inside
        for y in range(3):
            for z in range(3):

                def pack(x, carry, b=b, y=y, z=z):
                    rows = staged[x, y : y + 8, 7 + z : 15 + z, :]
                    copies[y, b, pl.ds(pl.multiple_of(x * 64, 64), 64), z * channels : (z + 1) * channels] = (
                        rows.reshape(64, channels).astype(jnp.bfloat16)
                    )
                    return carry

                lax.fori_loop(0, 10, pack, 0)


def gradient_kernel(lookup, hidden_t, left, grad, right, terms, copies, window, staged):
    bricks = grad.shape[0]
    channels = grad.shape[-1]
    half = channels // 2
    fill_copies(lookup, bricks, bricks, (left, grad, right), window, staged, copies)

    def gradient(i, carry):
        for z in range(3):
            summed = None
            for b in range(bricks):
                start = pl.multiple_of((i // 3) * 64, 64)
                rows = copies[i % 3, b, pl.ds(start, 512), z * channels : (z + 1) * channels]
                product = jnp.dot(hidden_t[b], rows, preferred_element_type=jnp.float32)
                summed = product if summed is None else summed + product
            tap = 26 - 3 * i - z
            terms[tap, 0] = summed[:, :half]
            terms[tap, 1] = summed[:, half:]
        return carry

    lax.fori_loop(0, 9, gradient, 0)


def blocks_kernel(lookup, left, hidden, right, copies, window, staged):
    fill_copies(lookup, hidden.shape[0], 0, (left, hidden, right), window, staged, copies)


def vmem_specs(count):
    return [pl.BlockSpec(memory_space=pltpu.VMEM)] * count


def block_scratch(bricks, channels):
    return [
        pltpu.VMEM((3 * bricks, 8, 8, 8, channels), jnp.float32),
        pltpu.VMEM((10, 10, 24, channels), jnp.float32),
    ]


def gradient_terms(lookup, hidden_t, grads):
    bricks, voxels, channels = grads[1].shape
    return pl.pallas_call(
        gradient_kernel,
        out_shape=(
            jax.ShapeDtypeStruct((27, 2, channels, channels // 2), jnp.float32),
            jax.ShapeDtypeStruct((3, bricks, 640, 3 * channels), jnp.bfloat16),
        ),
        in_specs=[pl.BlockSpec(memory_space=pltpu.SMEM)] + vmem_specs(4),
        out_specs=tuple(vmem_specs(2)),
        scratch_shapes=block_scratch(bricks, channels),
        compiler_params=pltpu.CompilerParams(vmem_limit_bytes=VMEM_BYTES),
        cost_estimate=pl.CostEstimate(
            flops=2 * 27 * bricks * voxels * channels * channels, bytes_accessed=60_000_000, transcendentals=0
        ),
    )(lookup, hidden_t, *grads)


def halo_blocks(lookup, hiddens):
    bricks, voxels, channels = hiddens[1].shape
    return pl.pallas_call(
        blocks_kernel,
        out_shape=jax.ShapeDtypeStruct((3, bricks, 640, 3 * channels), jnp.bfloat16),
        in_specs=[pl.BlockSpec(memory_space=pltpu.SMEM)] + vmem_specs(3),
        out_specs=vmem_specs(1)[0],
        scratch_shapes=block_scratch(bricks, channels),
        compiler_params=pltpu.CompilerParams(vmem_limit_bytes=VMEM_BYTES),
        cost_estimate=pl.CostEstimate(flops=0, bytes_accessed=30_000_000, transcendentals=0),
    )(lookup, *hiddens)


def scatter_kernel(
    scale, terms, features, active, hidden, grad, hid_source, weight_source, grad_source, weight_t_source,
    outputs, input_grad, result,
    hid_copies, weight, grad_copies, weight_t, total,
    own, r0, r1, r2, r3, r4, r5, arrive, local, send, recv,
):
    space, scene = lax.axis_index("space"), lax.axis_index("scene")
    core, x = scene % 2, scene // 2
    y, low, high = space % 2, (space // 2) % 2, space // 4
    partner = {
        "core": (space, scene + 1 - 2 * core),
        "x": (space, scene + 2 - 4 * x),
        "y": (space + 1 - 2 * y, scene),
        "low": (space + 2 - 4 * low, scene),
        "high": (space + 4 - 8 * high, scene),
    }
    barrier = pltpu.get_barrier_semaphore()
    for device in partner.values():
        pl.semaphore_signal(barrier, inc=1, device_id=device, device_id_type=MESH)
    pl.semaphore_wait(barrier, 5)

    moves = []
    for n, (source, target) in enumerate(
        ((hid_source, hid_copies), (weight_source, weight), (grad_source, grad_copies), (weight_t_source, weight_t))
    ):
        moves.append(pltpu.make_async_copy(source, target, local.at[n]))

    def convolve(n):
        task, part = n // 3, n % 3
        forward, b = task < bricks, task % bricks
        copied, matrix = (hid_copies, weight) if forward else (grad_copies, weight_t)
        if part == 0:
            if b == 0:
                for move in moves[:2] if forward else moves[2:]:
                    move.wait()
            total[...] = jnp.zeros_like(total)

        def step(i, carry):
            rows = copied[i % 3, b, pl.ds(pl.multiple_of((i // 3) * 64, 64), 512), :]
            total[...] += jnp.dot(rows, matrix[i], preferred_element_type=jnp.float32)
            return carry

        lax.fori_loop(3 * part, 3 * part + 3, step, 0)
        if part == 2 and forward:
            summed = (features[b].astype(jnp.float32) + total[...]) * active[b]
            outputs[b] = summed.astype(jnp.bfloat16)
        elif part == 2:
            passed = jnp.where(hidden[b].astype(jnp.float32) > 0, total[...], 0.0)
            input_grad[b] = (grad[b].astype(jnp.float32) + passed).astype(jnp.bfloat16)

    bricks = features.shape[0]
    chunks = r0.shape[0]
    copies, kept = {}, {}

    def begin(stage, k, source, target, axis):
        copy = pltpu.make_async_remote_copy(
            src_ref=source, dst_ref=target, send_sem=send.at[stage, k], recv_sem=recv.at[stage, k],
            device_id=partner[axis], device_id_type=MESH,
        )
        copy.start()
        copies[stage, k] = copy

    def advance(stage, k):
        taps = pl.ds(GROUP * k, GROUP)
        x_first = k % 2 == 0
        if stage == 0:
            begin(0, k, terms.at[taps, :, :, :, :, 1 - core], r0.at[k], "core")
            kept[k] = pltpu.make_async_copy(terms.at[taps, :, :, :, :, core], own.at[k], arrive.at[k])
            kept[k].start()
            return
        copies[stage - 1, k].wait_recv()
        if stage == 1:
            kept[k].wait()
            r0[k] = r0[k] + own[k]
            if x_first:
                begin(1, k, r0.at[k, :, 1 - x], r1.at[k], "x")
            else:
                begin(1, k, r0.at[k, :, :, :, :, 1 - y], r1.at[k], "y")
        elif stage == 2:
            if x_first:
                r1[k] = r1[k] + r0[k, :, x]
                begin(2, k, r1.at[k, :, :, :, 1 - y], r2.at[k], "y")
            else:
                r1[k] = r1[k] + r0[k, :, :, :, :, y]
                begin(2, k, r1.at[k, :, 1 - x], r2.at[k], "x")
        elif stage == 3:
            r2[k] = r2[k] + (r1[k, :, :, :, y] if x_first else r1[k, :, x])
            begin(3, k, r2.at[k, :, :, 1 - low], r3.at[k], "low")
        elif stage == 4:
            r3[k] = r3[k] + r2[k, :, :, low]
            begin(4, k, r3.at[k, :, 1 - high], r4.at[k], "high")
        elif stage == 5:
            r4[k] = r4[k] + r3[k, :, high]
            begin(5, k, r4.at[k], r5.at[k], "core")
        else:
            mine, other = r4[k] * scale, r5[k] * scale
            first = jnp.where(core == 0, mine, other)
            second = jnp.where(core == 0, other, mine)
            both = jnp.concatenate([first, second], axis=1)
            half = both.shape[-1] // 2
            result[taps] = jnp.where(core == 0, both[:, :, :half], both[:, :, half:])

    ahead = 2
    for k in range(min(ahead, chunks)):
        advance(0, k)
    for move in moves:
        move.start()
    parts = 6 * bricks
    for at in range(chunks + 5 * LAG):
        if at + ahead < chunks:
            advance(0, at + ahead)
        for stage in range(1, 7):
            k = at - LAG * (stage - 1)
            if 0 <= k < chunks:
                advance(stage, k)
        if DELAY <= at < DELAY + parts:
            convolve(at - DELAY)
    for n in range(chunks + 5 * LAG - DELAY, parts):
        convolve(n)
    for copy in copies.values():
        copy.wait_send()


def scatter_sum(terms, scale, fields, streamed):
    taps, _, channels, half = terms.shape
    features = fields[0]
    rows = channels // 16
    chunks = taps // GROUP
    f32 = jnp.float32
    tail = (rows, half)
    return pl.pallas_call(
        functools.partial(scatter_kernel, scale),
        out_shape=(
            jax.ShapeDtypeStruct(features.shape, jnp.bfloat16),
            jax.ShapeDtypeStruct(features.shape, jnp.bfloat16),
            jax.ShapeDtypeStruct((taps, 2 * rows, half // 2), f32),
        ),
        in_specs=[pl.BlockSpec(memory_space=pl.ANY)] + vmem_specs(4) + [pl.BlockSpec(memory_space=pl.ANY)] * 4,
        out_specs=tuple(vmem_specs(3)),
        scratch_shapes=[pltpu.VMEM(array.shape, array.dtype) for array in streamed]
        + [
            pltpu.VMEM(features.shape[1:], f32),
            pltpu.VMEM((chunks, GROUP, 2, 2, 2, 2) + tail, f32),
            pltpu.VMEM((chunks, GROUP, 2, 2, 2, 2) + tail, f32),
            pltpu.VMEM((chunks, GROUP, 2, 2, 2) + tail, f32),
            pltpu.VMEM((chunks, GROUP, 2, 2) + tail, f32),
            pltpu.VMEM((chunks, GROUP, 2) + tail, f32),
            pltpu.VMEM((chunks, GROUP) + tail, f32),
            pltpu.VMEM((chunks, GROUP) + tail, f32),
            pltpu.SemaphoreType.DMA((chunks,)),
            pltpu.SemaphoreType.DMA((4,)),
            pltpu.SemaphoreType.DMA((6, chunks)),
            pltpu.SemaphoreType.DMA((6, chunks)),
        ],
        compiler_params=pltpu.CompilerParams(
            collective_id=0, has_side_effects=True, vmem_limit_bytes=VMEM_BYTES
        ),
    )(terms.reshape(taps, 2, 2, 2, 2, 2, rows, half), *fields, *streamed)


def conv_kernel(features, active, hidden, grad, hid_copies, grad_copies, weight, weight_t, outputs, input_grad, total):
    for b in range(features.shape[0]):
        for copied, matrix in ((hid_copies, weight), (grad_copies, weight_t)):
            total[...] = jnp.zeros_like(total)

            def step(i, carry, b=b, copied=copied, matrix=matrix):
                rows = copied[i % 3, b, pl.ds(pl.multiple_of((i // 3) * 64, 64), 512), :]
                total[...] += jnp.dot(rows, matrix[i], preferred_element_type=jnp.float32)
                return carry

            lax.fori_loop(0, 9, step, 0)
            if copied is hid_copies:
                summed = (features[b].astype(jnp.float32) + total[...]) * active[b]
                outputs[b] = summed.astype(jnp.bfloat16)
            else:
                kept = jnp.where(hidden[b].astype(jnp.float32) > 0, total[...], 0.0)
                input_grad[b] = (grad[b].astype(jnp.float32) + kept).astype(jnp.bfloat16)


def convolve_alone(fields, streamed):
    shape = jax.ShapeDtypeStruct(fields[0].shape, jnp.bfloat16)
    hid_copies, weight, grad_copies, weight_t = streamed
    return pl.pallas_call(
        conv_kernel,
        out_shape=(shape, shape),
        in_specs=vmem_specs(8),
        out_specs=tuple(vmem_specs(2)),
        scratch_shapes=[pltpu.VMEM(fields[0].shape[1:], jnp.float32)],
        compiler_params=pltpu.CompilerParams(vmem_limit_bytes=VMEM_BYTES),
    )(*fields, hid_copies, grad_copies, weight, weight_t)


def per_device(features, cotangent, weight, counts, neighbours, occupancy):
    shape = features.shape
    bricks, extent, channels = shape[1], shape[2], shape[-1]
    voxels = extent * extent * extent
    feats = features.reshape(bricks, voxels, channels)
    slot_live = (jnp.arange(bricks, dtype=jnp.int32) < counts[0, 0]).astype(jnp.int32)
    active = (occupancy[0] * slot_live[:, None]).reshape(bricks, voxels, 1)
    live = active.astype(jnp.float32)
    hidden, grad, packed = prepare(
        feats, cotangent.reshape(bricks, voxels, channels), live
    )
    left, right = both_sides(packed)
    first_id = (lax.axis_index("space") - 1) * bricks
    linked = neighbours[0]
    local_ids = jnp.where(linked >= 0, linked - first_id, -1)
    centre = (bricks + jnp.arange(bricks, dtype=jnp.int32))[:, None]
    lookup = jnp.concatenate([local_ids[:, :13], centre, local_ids[:, 13:]], axis=1)
    weight_t = weight[::-1].swapaxes(1, 2).reshape(9, 3 * channels, channels)
    terms, grad_copies = gradient_terms(lookup, hidden.swapaxes(1, 2), (left, grad, right))
    hid_copies = halo_blocks(lookup, (left, hidden, right))
    fields = (feats, live, hidden, grad)
    streamed = (hid_copies, weight.reshape(9, 3 * channels, channels), grad_copies, weight_t)
    space, scene = lax.axis_size("space"), lax.axis_size("scene")
    scale = float(scene * space * bricks * voxels) ** (-0.5)
    if (space, scene) == (8, 4):
        outputs, input_grad, weight_grad = scatter_sum(terms, scale, fields, streamed)
    else:
        outputs, input_grad = convolve_alone(fields, streamed)
        whole = jnp.concatenate([terms[:, 0], terms[:, 1]], axis=2) * scale
        across = lax.psum_scatter(whole, "scene", scatter_dimension=2, tiled=True)
        weight_grad = lax.psum_scatter(across, "space", scatter_dimension=1, tiled=True)
    return outputs.reshape(shape), input_grad.reshape(shape), weight_grad


def solution(mesh):
    field = P("scene", "space", None, None, None, None)
    in_specs = (field, field, P(), P("scene", "space"), P("scene", "space", None), P("scene", "space", None))
    out_specs = (field, field, P(None, "space", "scene"))
    return jax.shard_map(per_device, mesh=mesh, in_specs=in_specs, out_specs=out_specs, check_vma=False)
```

```python
import functools

import jax
import jax.numpy as jnp
from jax import lax
from jax.experimental import pallas as pl
from jax.experimental.pallas import tpu as pltpu
from jax.sharding import PartitionSpec as P

MESH = pl.DeviceIdType.MESH
VMEM_BYTES = 56 * 1024 * 1024
GROUP = 3
LAG = 3


def both_sides(cells):
    count = lax.axis_size("space")
    ends = count - 1
    left = lax.ppermute(cells, "space", [(i, i + 1) for i in range(ends)])
    right = lax.ppermute(cells, "space", [(i + 1, i) for i in range(ends)])
    return left, right


def spans(shift):
    if shift < 0:
        return slice(7, 8), slice(0, 1)
    if shift == 0:
        return slice(0, 8), slice(1, 9)
    return slice(0, 1), slice(9, 10)


def spans_z(shift):
    if shift < 0:
        return slice(7, 8), slice(7, 8)
    if shift == 0:
        return slice(0, 8), slice(8, 16)
    return slice(0, 1), slice(16, 17)


def prepare_kernel(features, cotangent, active, hidden, grad, packed_hidden, packed_grad, block):
    channels = block.shape[-1]
    for b in range(features.shape[0]):
        for source, target, packed in ((cotangent, grad, packed_grad), (features, hidden, packed_hidden)):

            def mask(x, carry, source=source, target=target, b=b):
                at = pl.ds(pl.multiple_of(x * 64, 64), 64)
                rows = source[b, at, :].astype(jnp.float32)
                if source is features:
                    rows = jnp.maximum(rows, 0)
                rows = rows * active[b, at, :]
                target[b, at, :] = rows.astype(jnp.bfloat16)
                block[x] = rows.reshape(8, 8, channels)
                return carry

            lax.fori_loop(0, 8, mask, 0)
            for n, x in enumerate((0, 7)):
                packed[b, 64 * n : 64 * n + 64, :] = block[x].reshape(64, channels).astype(jnp.bfloat16)
            for x in range(1, 7):
                faces_y = jnp.concatenate([block[x, 0], block[x, 7]], axis=0)
                packed[b, 112 + 16 * x : 128 + 16 * x, :] = faces_y.astype(jnp.bfloat16)
                faces_z = jnp.concatenate([block[x, :, 0, :], block[x, :, 7, :]], axis=0)
                packed[b, 208 + 16 * x : 224 + 16 * x, :] = faces_z.astype(jnp.bfloat16)


def prepare(features, cotangent, active):
    bricks, _, channels = features.shape
    whole = jax.ShapeDtypeStruct(features.shape, jnp.bfloat16)
    surface = jax.ShapeDtypeStruct((bricks, 320, channels), jnp.bfloat16)
    return pl.pallas_call(
        prepare_kernel,
        out_shape=(whole, whole, surface, surface),
        in_specs=vmem_specs(3),
        out_specs=tuple(vmem_specs(4)),
        scratch_shapes=[pltpu.VMEM((8, 8, 8, channels), jnp.float32)],
        compiler_params=pltpu.CompilerParams(vmem_limit_bytes=VMEM_BYTES),
    )(features, cotangent, active)


def unpack(packed, b, at, window):
    channels = window.shape[-1]
    for n, x in enumerate((0, 7)):
        rows = packed[b, 64 * n : 64 * n + 64, :].astype(jnp.float32)
        window[at, x] = rows.reshape(8, 8, channels)
    for x in range(1, 7):
        faces_y = packed[b, 112 + 16 * x : 128 + 16 * x, :].astype(jnp.float32)
        faces_z = packed[b, 208 + 16 * x : 224 + 16 * x, :].astype(jnp.float32)
        window[at, x, 0], window[at, x, 7] = faces_y[:8], faces_y[8:]
        window[at, x, :, 0, :], window[at, x, :, 7, :] = faces_z[:8], faces_z[8:]


def fill_copies(lookup, bricks, sides, window, staged, copies):
    channels = staged.shape[-1]
    left, own, right = sides
    for b in range(bricks):
        unpack(left, b, b, window)
        unpack(right, b, 2 * bricks + b, window)

        def widen(x, carry, b=b):
            rows = own[b, pl.ds(pl.multiple_of(x * 64, 64), 64), :]
            window[bricks + b, x] = rows.astype(jnp.float32).reshape(8, 8, channels)
            return carry

        lax.fori_loop(0, 8, widen, 0)
    for b in range(bricks):
        for sx in (-1, 0, 1):
            for sy in (-1, 0, 1):
                for sz in (-1, 0, 1):
                    (from_x, to_x), (from_y, to_y), (from_z, to_z) = spans(sx), spans(sy), spans_z(sz)
                    if sx == sy == sz == 0:
                        staged[to_x, to_y, to_z, :] = window[bricks + b, from_x, from_y, from_z, :]
                        continue
                    at = lookup[b, 9 * (sx + 1) + 3 * (sy + 1) + sz + 1]
                    inside = (at >= 0).astype(jnp.float32)
                    taken = window[jnp.maximum(at, 0), from_x, from_y, from_z, :]
                    staged[to_x, to_y, to_z, :] = taken * inside
        for y in range(3):
            for z in range(3):

                def pack(x, carry, b=b, y=y, z=z):
                    rows = staged[x, y : y + 8, 7 + z : 15 + z, :]
                    copies[y, b, pl.ds(pl.multiple_of(x * 64, 64), 64), z * channels : (z + 1) * channels] = (
                        rows.reshape(64, channels).astype(jnp.bfloat16)
                    )
                    return carry

                lax.fori_loop(0, 10, pack, 0)


def gradient_kernel(lookup, hidden_t, left, grad, right, terms, copies, window, staged):
    bricks = grad.shape[0]
    channels = grad.shape[-1]
    half = channels // 2
    fill_copies(lookup, bricks, (left, grad, right), window, staged, copies)

    def gradient(i, carry):
        for z in range(3):
            summed = None
            for b in range(bricks):
                start = pl.multiple_of((i // 3) * 64, 64)
                rows = copies[i % 3, b, pl.ds(start, 512), z * channels : (z + 1) * channels]
                product = jnp.dot(hidden_t[b], rows, preferred_element_type=jnp.float32)
                summed = product if summed is None else summed + product
            tap = 26 - 3 * i - z
            terms[tap, 0] = summed[:, :half]
            terms[tap, 1] = summed[:, half:]
        return carry

    lax.fori_loop(0, 9, gradient, 0)


def blocks_kernel(lookup, left, hidden, right, copies, window, staged):
    fill_copies(lookup, hidden.shape[0], (left, hidden, right), window, staged, copies)


def vmem_specs(count):
    return [pl.BlockSpec(memory_space=pltpu.VMEM)] * count


def block_scratch(bricks, channels):
    return [
        pltpu.VMEM((3 * bricks, 8, 8, 8, channels), jnp.float32),
        pltpu.VMEM((10, 10, 24, channels), jnp.float32),
    ]


def gradient_terms(lookup, hidden_t, grads):
    bricks, voxels, channels = grads[1].shape
    return pl.pallas_call(
        gradient_kernel,
        out_shape=(
            jax.ShapeDtypeStruct((27, 2, channels, channels // 2), jnp.float32),
            jax.ShapeDtypeStruct((3, bricks, 640, 3 * channels), jnp.bfloat16),
        ),
        in_specs=[pl.BlockSpec(memory_space=pltpu.SMEM)] + vmem_specs(4),
        out_specs=tuple(vmem_specs(2)),
        scratch_shapes=block_scratch(bricks, channels),
        compiler_params=pltpu.CompilerParams(vmem_limit_bytes=VMEM_BYTES),
        cost_estimate=pl.CostEstimate(
            flops=2 * 27 * bricks * voxels * channels * channels, bytes_accessed=60_000_000, transcendentals=0
        ),
    )(lookup, hidden_t, *grads)


def halo_blocks(lookup, hiddens):
    bricks, voxels, channels = hiddens[1].shape
    return pl.pallas_call(
        blocks_kernel,
        out_shape=jax.ShapeDtypeStruct((3, bricks, 640, 3 * channels), jnp.bfloat16),
        in_specs=[pl.BlockSpec(memory_space=pltpu.SMEM)] + vmem_specs(3),
        out_specs=vmem_specs(1)[0],
        scratch_shapes=block_scratch(bricks, channels),
        compiler_params=pltpu.CompilerParams(vmem_limit_bytes=VMEM_BYTES),
        cost_estimate=pl.CostEstimate(flops=0, bytes_accessed=30_000_000, transcendentals=0),
    )(lookup, *hiddens)


def scatter_kernel(
    scale, terms, features, active, hidden, grad, hid_source, weight_source, grad_source, weight_t_source,
    outputs, input_grad, result,
    hid_copies, weight, grad_copies, weight_t, total,
    r0, r1, r2, r3, r4, r5, local, send, recv,
):
    space, scene = lax.axis_index("space"), lax.axis_index("scene")
    core, x = scene % 2, scene // 2
    y, low, high = space % 2, (space // 2) % 2, space // 4
    partner = {
        "core": (space, scene + 1 - 2 * core),
        "x": (space, scene + 2 - 4 * x),
        "y": (space + 1 - 2 * y, scene),
        "low": (space + 2 - 4 * low, scene),
        "high": (space + 4 - 8 * high, scene),
    }
    barrier = pltpu.get_barrier_semaphore()
    for device in partner.values():
        pl.semaphore_signal(barrier, inc=1, device_id=device, device_id_type=MESH)
    pl.semaphore_wait(barrier, 5)

    moves = []
    for n, (source, target) in enumerate(
        ((hid_source, hid_copies), (weight_source, weight), (grad_source, grad_copies), (weight_t_source, weight_t))
    ):
        moves.append(pltpu.make_async_copy(source, target, local.at[n]))
        moves[n].start()

    def convolve(n):
        task, part = n // 3, n % 3
        forward, b = task < bricks, task % bricks
        copied, matrix = (hid_copies, weight) if forward else (grad_copies, weight_t)
        if part == 0:
            if b == 0:
                for move in moves[:2] if forward else moves[2:]:
                    move.wait()
            total[...] = jnp.zeros_like(total)

        def step(i, carry):
            rows = copied[i % 3, b, pl.ds(pl.multiple_of((i // 3) * 64, 64), 512), :]
            total[...] += jnp.dot(rows, matrix[i], preferred_element_type=jnp.float32)
            return carry

        lax.fori_loop(3 * part, 3 * part + 3, step, 0)
        if part == 2 and forward:
            summed = (features[b].astype(jnp.float32) + total[...]) * active[b]
            outputs[b] = summed.astype(jnp.bfloat16)
        elif part == 2:
            kept = jnp.where(hidden[b].astype(jnp.float32) > 0, total[...], 0.0)
            input_grad[b] = (grad[b].astype(jnp.float32) + kept).astype(jnp.bfloat16)

    bricks = features.shape[0]
    chunks = r0.shape[0]
    copies = {}

    def begin(stage, k, source, target, axis):
        copy = pltpu.make_async_remote_copy(
            src_ref=source, dst_ref=target, send_sem=send.at[stage, k], recv_sem=recv.at[stage, k],
            device_id=partner[axis], device_id_type=MESH,
        )
        copy.start()
        copies[stage, k] = copy

    def advance(stage, k):
        taps = pl.ds(GROUP * k, GROUP)
        x_first = k % 2 == 0
        if stage == 0:
            begin(0, k, terms.at[taps, :, :, :, :, 1 - core], r0.at[k], "core")
            return
        copies[stage - 1, k].wait_recv()
        if stage == 1:
            r0[k] = r0[k] + terms[taps, :, :, :, :, core]
            if x_first:
                begin(1, k, r0.at[k, :, 1 - x], r1.at[k], "x")
            else:
                begin(1, k, r0.at[k, :, :, :, :, 1 - y], r1.at[k], "y")
        elif stage == 2:
            if x_first:
                r1[k] = r1[k] + r0[k, :, x]
                begin(2, k, r1.at[k, :, :, :, 1 - y], r2.at[k], "y")
            else:
                r1[k] = r1[k] + r0[k, :, :, :, :, y]
                begin(2, k, r1.at[k, :, 1 - x], r2.at[k], "x")
        elif stage == 3:
            r2[k] = r2[k] + (r1[k, :, :, :, y] if x_first else r1[k, :, x])
            begin(3, k, r2.at[k, :, :, 1 - low], r3.at[k], "low")
        elif stage == 4:
            r3[k] = r3[k] + r2[k, :, :, low]
            begin(4, k, r3.at[k, :, 1 - high], r4.at[k], "high")
        elif stage == 5:
            r4[k] = r4[k] + r3[k, :, high]
            begin(5, k, r4.at[k], r5.at[k], "core")
        else:
            mine, other = r4[k] * scale, r5[k] * scale
            first = jnp.where(core == 0, mine, other)
            second = jnp.where(core == 0, other, mine)
            both = jnp.concatenate([first, second], axis=1)
            half = both.shape[-1] // 2
            result[taps] = jnp.where(core == 0, both[:, :, :half], both[:, :, half:])

    ahead = 2
    for k in range(min(ahead, chunks)):
        advance(0, k)
    parts = 6 * bricks
    for at in range(chunks + 5 * LAG):
        if at + ahead < chunks:
            advance(0, at + ahead)
        for stage in range(1, 7):
            k = at - LAG * (stage - 1)
            if 0 <= k < chunks:
                advance(stage, k)
        if 1 <= at <= parts:
            convolve(at - 1)
    for n in range(chunks + 5 * LAG - 1, parts):
        convolve(n)
    for copy in copies.values():
        copy.wait_send()


def scatter_sum(terms, scale, fields, streamed):
    taps, _, channels, half = terms.shape
    features = fields[0]
    rows = channels // 16
    chunks = taps // GROUP
    f32 = jnp.float32
    tail = (rows, half)
    return pl.pallas_call(
        functools.partial(scatter_kernel, scale),
        out_shape=(
            jax.ShapeDtypeStruct(features.shape, jnp.bfloat16),
            jax.ShapeDtypeStruct(features.shape, jnp.bfloat16),
            jax.ShapeDtypeStruct((taps, 2 * rows, half // 2), f32),
        ),
        in_specs=vmem_specs(5) + [pl.BlockSpec(memory_space=pl.ANY)] * 4,
        out_specs=tuple(vmem_specs(3)),
        scratch_shapes=[pltpu.VMEM(array.shape, array.dtype) for array in streamed]
        + [
            pltpu.VMEM(features.shape[1:], f32),
            pltpu.VMEM((chunks, GROUP, 2, 2, 2, 2) + tail, f32),
            pltpu.VMEM((chunks, GROUP, 2, 2, 2) + tail, f32),
            pltpu.VMEM((chunks, GROUP, 2, 2) + tail, f32),
            pltpu.VMEM((chunks, GROUP, 2) + tail, f32),
            pltpu.VMEM((chunks, GROUP) + tail, f32),
            pltpu.VMEM((chunks, GROUP) + tail, f32),
            pltpu.SemaphoreType.DMA((4,)),
            pltpu.SemaphoreType.DMA((6, chunks)),
            pltpu.SemaphoreType.DMA((6, chunks)),
        ],
        compiler_params=pltpu.CompilerParams(
            collective_id=0, has_side_effects=True, vmem_limit_bytes=VMEM_BYTES
        ),
    )(terms.reshape(taps, 2, 2, 2, 2, 2, rows, half), *fields, *streamed)


def conv_kernel(features, active, hidden, grad, hid_copies, grad_copies, weight, weight_t, outputs, input_grad, total):
    for b in range(features.shape[0]):
        for copied, matrix in ((hid_copies, weight), (grad_copies, weight_t)):
            total[...] = jnp.zeros_like(total)

            def step(i, carry, b=b, copied=copied, matrix=matrix):
                rows = copied[i % 3, b, pl.ds(pl.multiple_of((i // 3) * 64, 64), 512), :]
                total[...] += jnp.dot(rows, matrix[i], preferred_element_type=jnp.float32)
                return carry

            lax.fori_loop(0, 9, step, 0)
            if copied is hid_copies:
                summed = (features[b].astype(jnp.float32) + total[...]) * active[b]
                outputs[b] = summed.astype(jnp.bfloat16)
            else:
                kept = jnp.where(hidden[b].astype(jnp.float32) > 0, total[...], 0.0)
                input_grad[b] = (grad[b].astype(jnp.float32) + kept).astype(jnp.bfloat16)


def convolve_alone(fields, streamed):
    shape = jax.ShapeDtypeStruct(fields[0].shape, jnp.bfloat16)
    hid_copies, weight, grad_copies, weight_t = streamed
    return pl.pallas_call(
        conv_kernel,
        out_shape=(shape, shape),
        in_specs=vmem_specs(8),
        out_specs=tuple(vmem_specs(2)),
        scratch_shapes=[pltpu.VMEM(fields[0].shape[1:], jnp.float32)],
        compiler_params=pltpu.CompilerParams(vmem_limit_bytes=VMEM_BYTES),
    )(*fields, hid_copies, grad_copies, weight, weight_t)


def per_device(features, cotangent, weight, counts, neighbours, occupancy):
    shape = features.shape
    bricks, extent, channels = shape[1], shape[2], shape[-1]
    voxels = extent * extent * extent
    feats = features.reshape(bricks, voxels, channels)
    slot_live = (jnp.arange(bricks, dtype=jnp.int32) < counts[0, 0]).astype(jnp.int32)
    active = (occupancy[0] * slot_live[:, None]).reshape(bricks, voxels, 1)
    live = active.astype(jnp.float32)
    hidden, grad, packed_hidden, packed_grad = prepare(
        feats, cotangent.reshape(bricks, voxels, channels), live
    )
    grad_left, grad_right = both_sides(packed_grad)
    hid_left, hid_right = both_sides(packed_hidden)
    first_id = (lax.axis_index("space") - 1) * bricks
    linked = neighbours[0]
    local_ids = jnp.where(linked >= 0, linked - first_id, -1)
    centre = (bricks + jnp.arange(bricks, dtype=jnp.int32))[:, None]
    lookup = jnp.concatenate([local_ids[:, :13], centre, local_ids[:, 13:]], axis=1)
    weight_t = weight[::-1].swapaxes(1, 2).reshape(9, 3 * channels, channels)
    terms, grad_copies = gradient_terms(lookup, hidden.swapaxes(1, 2), (grad_left, grad, grad_right))
    hid_copies = halo_blocks(lookup, (hid_left, hidden, hid_right))
    fields = (feats, live, hidden, grad)
    streamed = (hid_copies, weight.reshape(9, 3 * channels, channels), grad_copies, weight_t)
    space, scene = lax.axis_size("space"), lax.axis_size("scene")
    scale = float(scene * space * bricks * voxels) ** (-0.5)
    if (space, scene) == (8, 4):
        outputs, input_grad, weight_grad = scatter_sum(terms, scale, fields, streamed)
    else:
        outputs, input_grad = convolve_alone(fields, streamed)
        whole = jnp.concatenate([terms[:, 0], terms[:, 1]], axis=2) * scale
        across = lax.psum_scatter(whole, "scene", scatter_dimension=2, tiled=True)
        weight_grad = lax.psum_scatter(across, "space", scatter_dimension=1, tiled=True)
    return outputs.reshape(shape), input_grad.reshape(shape), weight_grad


def solution(mesh):
    field = P("scene", "space", None, None, None, None)
    in_specs = (field, field, P(), P("scene", "space"), P("scene", "space", None), P("scene", "space", None))
    out_specs = (field, field, P(None, "space", "scene"))
    return jax.shard_map(per_device, mesh=mesh, in_specs=in_specs, out_specs=out_specs, check_vma=False)
```
